256 devices in a mesh: dp: 16 (over x, y_hi, core), mp: 16 (over y_lo, z).
Axes of the slice: x: 4, y: 4 (y_hi: 2, y_lo: 2; y = y_hi * 2 + y_lo), z: 8, core: 2. Of those that a mesh axis runs over, the one named last changes fastest.
Arguments:
- out_grads: bfloat16 [2048, 8192], P('dp', 'mp'), may hold values from -6 to 6
- basis: bfloat16 [8192, 8192], P('dp', 'mp'), may hold values from -0.0625 to 0.0625
- left_factors: bfloat16 [8192, 4096], P('mp', 'dp'), may hold values from -0.0625 to 0.0625
- right_factors: bfloat16 [28672, 4096], P('mp', 'dp'), may hold values from -0.03125 to 0.03125
- activations: bfloat16 [2048, 28672], P('dp', 'mp'), may hold values from -6 to 6
- spans: int32 [16, 5], P('dp'), may hold values from 1 to 64, 128 in all within a row
Outputs:
- scores: float32 [64, 128], P('dp', 'mp')
The draws below stay inside these ranges and needn't reach their ends.
Inputs may be any that keep to these rules, and one draw needn't show every extreme that they name: `spans`: each row sums to 128; every entry is at least 1, and the largest entry of each row is exactly 64.
All inputs are finite; a program needn't handle non-finite values.
Results may differ from the reference program's by a relative error of at most 0.0029.
Values may be sent and summed in bfloat16 or wider, within the bound.
A program may use at most 128 MiB of HBM per device.

```python
import math
import jax
import jax.numpy as jnp
import numpy as np
from jax import lax

IN = 28672
OUT = 8192
NQ = 128
RANK = 32
TOK_DEV = 128
SEQ_DEV = 4
MOST = 64
QR = 4096
TOKENS = 2048
NSEQ = 64
N_DP = 16


def block_scale(stream_key, shape, cuts, smallest, high):
    loudness, own = 1.0, jax.random.fold_in(stream_key, 6)
    for dim, parts in cuts:
        steps = jnp.exp(jax.random.uniform(jax.random.fold_in(own, dim), (parts,), jnp.float32, smallest / len(cuts), high / len(cuts)))
        loudness = loudness * jnp.repeat(steps, shape[dim] // parts).reshape([-1 if axis == dim else 1 for axis in range(len(shape))])
    return loudness


def split_up(number_of, total, bound, lean):
    weights = [(1 << 20) // math.isqrt(rank ** lean) + 1 for rank in range(2, number_of + 1)]
    surplus, given = total - bound - (number_of - 1), [1] * (number_of - 1)
    while surplus > 0:
        movable = [i for i in range(number_of - 1) if given[i] < bound]
        mass, remaining = sum([weights[i] for i in movable]), surplus
        for i in movable:
            addition = min(bound - given[i], max(1, remaining * weights[i] // mass), surplus)
            given[i] = given[i] + addition
            surplus = surplus - addition
    return np.array([bound] + given)


def uneven_parts(stream_key, number_of, total, limit, skew):
    if number_of == 2:
        one = jax.random.randint(stream_key, (), max(1, total - limit), min(limit, total - 1) + 1)
        return jnp.stack([one, total - one])
    sizes = jnp.asarray(split_up(number_of, total, limit, skew), jnp.int32)
    twos = (number_of - 1) // 2
    source_of, sink = sizes[1:1 + 2 * twos:2], sizes[2:2 + 2 * twos:2]
    room = jnp.minimum(source_of - 1, limit - sink)
    passed = jax.random.randint(jax.random.fold_in(stream_key, 1), (twos,), 0, 1 << 20) % (room + 1)
    sizes = sizes.at[1:1 + 2 * twos:2].set(source_of - passed).at[2:2 + 2 * twos:2].set(sink + passed)
    return sizes[jax.random.permutation(jax.random.fold_in(stream_key, 2), number_of)]


def noise(stream_key, extent, width, most, pieces=(), kind=jnp.bfloat16):
    loudness = block_scale(stream_key, extent, pieces, -0.22, 0.18) if pieces else 1.0
    values = jax.random.normal(stream_key, extent, jnp.float32) * width * loudness
    return jnp.minimum(jnp.maximum(values, -most), most).astype(kind)


def setup_inputs(seed: int = 0) -> dict:
    arg_keys = jax.random.split(jax.random.key(seed), 7)
    return {
        "out_grads": noise(arg_keys[0], (TOKENS, OUT), 1.0, 6.0, ((0, 16), (1, 16))),
        "basis": noise(arg_keys[1], (OUT, OUT), OUT ** -0.5, 0.0625, ((0, 16), (1, 16))),
        "left_factors": noise(arg_keys[2], (OUT, QR), OUT ** -0.5, 0.0625, ((0, 16), (1, 16))),
        "right_factors": noise(arg_keys[3], (IN, QR), IN ** -0.5, 0.03125, ((0, 16), (1, 16))),
        "activations": noise(arg_keys[4], (TOKENS, IN), 1.0, 6.0, ((0, 16), (1, 16))),
        "spans": jax.vmap(lambda own: uneven_parts(own, SEQ_DEV + 1, TOK_DEV, MOST, 1))(jax.random.split(arg_keys[5], N_DP)).reshape((N_DP, SEQ_DEV + 1)).astype(jnp.int32),
    }


def reference(out_grads, basis, left_factors, right_factors, activations, spans):
    rotated = jnp.dot(out_grads, basis, preferred_element_type=jnp.float32).astype(jnp.bfloat16)
    left = jnp.dot(rotated, left_factors, preferred_element_type=jnp.float32)
    right = jnp.dot(activations, right_factors, preferred_element_type=jnp.float32)
    per_token = (left * right).reshape(TOKENS, NQ, RANK).sum(axis=2)
    per_token = per_token.reshape(N_DP, TOK_DEV, NQ)
    lengths = spans[:, :SEQ_DEV]
    starts = jnp.cumsum(spans, axis=1)[:, :SEQ_DEV] - lengths
    slots = jnp.arange(TOK_DEV, dtype=jnp.int32)
    inside = (slots[None, None, :] >= starts[:, :, None]) & (slots[None, None, :] < (starts + lengths)[:, :, None])
    members = inside.astype(jnp.float32)
    summed = jnp.einsum('isk,ikq->isq', members, per_token, precision=lax.Precision.HIGHEST)
    scale = 1.0 / jnp.sqrt(jnp.float32(RANK * TOK_DEV))
    return summed.reshape(NSEQ, NQ) * scale
```

```python
import functools

import jax
import jax.numpy as jnp
from jax import lax
from jax.experimental import pallas as pl
from jax.experimental.pallas import tpu as pltpu
from jax.sharding import PartitionSpec as P

RANK = 32
TOK_DEV = 128
SEQ_DEV = 4
MESH = pl.DeviceIdType.MESH
BF16, F32 = jnp.bfloat16, jnp.float32

NX, NZ, NM = 4, 8, 16
T, O, E, C, I = 128, 512, 512, 256, 1792


def kernel(g_in, b_in, l_in, r_in, a_in, sp, out, gbuf, bbuf, lbuf, rbuf, abuf, prot, rprot, xrot, pbuf, pown, rsbuf, rfull,
           left, ends, sbuf, srecv, fin_s, fin_r, loc, ss, rs):
    d, m = lax.axis_index("dp"), lax.axis_index("mp")
    x, yh, c = d // 4, (d // 2) % 2, d % 2
    yl, z = m // NZ, m % NZ

    def dev(x_=None, yh_=None, c_=None, yl_=None, z_=None):
        pick = lambda new, old: old if new is None else new
        return (4 * pick(x_, x) + 2 * pick(yh_, yh) + pick(c_, c), NZ * pick(yl_, yl) + pick(z_, z))

    xs = [(x + k) % NX for k in range(NX)]
    zr, zl = (z + 1) % NZ, (z + NZ - 1) % NZ
    sibling, across, beside = dev(c_=1 - c), dev(yh_=1 - yh), dev(yl_=1 - yl)
    bit = (m // 2) % 2
    swap_m = m + 2 - 4 * bit
    swapped = (4 * x + 2 * (1 - yh) + c, swap_m)
    turn = (4 * (m // 4) + 2 * yh + c, 4 * x + m % 4)
    turns = x != m // 4

    def greet(to):
        pl.semaphore_signal(pltpu.get_barrier_semaphore(), inc=1, device_id=to, device_id_type=MESH)

    for k in (1, 2, 3):
        greet(dev(x_=xs[k]))
    for to in (sibling, across, swapped):
        greet(to)

    @pl.loop(1, NM)
    def _(k):
        greet((d, (m + k) % NM))

    pl.when(turns)(lambda: greet(turn))
    pl.semaphore_wait(pltpu.get_barrier_semaphore(), jnp.where(turns, 22, 21))

    used = [0]

    def take(n=1):
        used[0] += n
        return used[0] - n

    sent = []

    def copy(src, dst, to, sem, sem_there=None):
        sem_there = sem if sem_there is None else sem_there
        return pltpu.make_async_remote_copy(
            src_ref=src, dst_ref=dst, send_sem=ss.at[sem], recv_sem=rs.at[sem_there], device_id=to, device_id_type=MESH
        )

    def send(src, dst, to, sem):
        cp = copy(src, dst, to, sem)
        cp.start()
        sent.append(cp)

    def arrived(dst, sem):
        copy(dst, dst, sibling, sem).wait_recv()

    def gslot(mm, lo=0, n=T):
        return gbuf.at[(mm // 4) * 2 + mm % 2, pl.ds(((mm // 2) % 2) * T + lo, n)]

    def fslot(mm, lo=0, n=T):
        return rfull.at[mm, pl.ds(lo, n)]

    def arow(xx, lo=0, n=T):
        return abuf.at[pl.ds(xx * T + lo, n)]

    def bslot(xx, cc, lo=0, n=O):
        return bbuf.at[xx * 2 + cc, pl.ds(lo, n)]

    def spread(slot):
        sem_pair, sem = take(), take(16)
        half = T // 2

        def at(stream, direction, step):
            return sem + stream * 8 + direction * 4 + step

        def stage(stream, step):
            row = yl if stream == 0 else 1 - yl
            for direction, (to, sign) in enumerate(((zr, -1), (zl, 1))):
                origin = row * NZ + (z + sign * step + NZ) % NZ
                lo, n = (0, T) if step < 3 else (half * direction, half)
                send(slot(origin, lo, n), slot(origin, lo, n), dev(z_=to), at(stream, direction, step))

        def landed(stream, step):
            row = yl if stream == 0 else 1 - yl
            for direction, sign in ((0, -1), (1, 1)):
                origin = row * NZ + (z + sign * (step + 1) + NZ) % NZ
                lo, n = (0, T) if step < 3 else (half * direction, half)
                arrived(slot(origin, lo, n), at(stream, direction, step))

        def begin():
            send(slot(m), slot(m), beside, sem_pair)
            stage(0, 0)

        def second():
            arrived(slot((1 - yl) * NZ + z), sem_pair)
            stage(1, 0)

        def step(k):
            for stream in (0, 1):
                landed(stream, k)
                if k < 3:
                    stage(stream, k + 1)

        return begin, second, step

    places = [(a_in, arow(x)), (b_in, bslot(x, c)), (l_in, lbuf.at[yh * 2 + c]), (r_in, rbuf.at[yh * 2 + c])]
    own = [pltpu.make_async_copy(src, dst, loc.at[i]) for i, (src, dst) in enumerate(places)]
    own_g = pltpu.make_async_copy(g_in, gslot(m), loc.at[4])
    sem_g = take()
    move_g = copy(g_in, gslot(swap_m), swapped, sem_g)
    moves = yh != bit
    pl.when(moves)(lambda: move_g.start())
    pl.when(jnp.logical_not(moves))(lambda: own_g.start())

    def ring(src, slot, size):
        sem = take(4)
        half = size // 2

        def begin():
            send(src, slot(x, 0, size), dev(x_=xs[1]), sem)
            send(src, slot(x, 0, size), dev(x_=xs[3]), sem + 1)

        def first():
            arrived(slot(xs[3], 0, size), sem)
            send(slot(xs[3], 0, half), slot(xs[3], 0, half), dev(x_=xs[1]), sem + 2)
            arrived(slot(xs[1], 0, size), sem + 1)
            send(slot(xs[1], half, half), slot(xs[1], half, half), dev(x_=xs[3]), sem + 3)

        def last():
            arrived(slot(xs[2], 0, half), sem + 2)
            arrived(slot(xs[2], half, half), sem + 3)

        return begin, first, last

    a_begin, a_first, a_last = ring(a_in, arow, T)
    b_begin, b_first, b_last = ring(b_in, lambda xx, lo, n: bslot(xx, c, lo, n), O)
    a_begin()
    sem_r, sem_l, sem_rd, sem_ld, sem_bd = take(), take(), take(2), take(2), take(4)
    mine, other = yh * 2 + c, (1 - yh) * 2 + c
    send(r_in, rbuf.at[mine], across, sem_r)
    send(r_in, rbuf.at[mine], sibling, sem_rd)
    send(b_in, bslot(x, c), sibling, sem_bd)
    send(l_in, lbuf.at[mine], sibling, sem_ld)
    for cp in own:
        cp.start()

    row = lax.broadcasted_iota(jnp.int32, (8, 128), 0)
    tile = jnp.zeros((8, 128), jnp.int32)
    end = 0
    for k in range(SEQ_DEV):
        end = end + sp[0, k]
        tile = jnp.where(row == k, end, tile)
    ends[x] = tile
    sem_e = take(3)
    for k in (1, 2, 3):
        send(ends.at[x], ends.at[x], dev(x_=xs[k]), sem_e + k - 1)

    pl.when(moves)(lambda: copy(g_in, gslot(m), swapped, sem_g).wait_recv())
    pl.when(jnp.logical_not(moves))(lambda: own_g.wait())
    g_begin, g_second, g_step = spread(gslot)
    g_begin()
    g_second()
    g_step(0)
    a_first()
    b_begin()
    g_step(1)

    sem_rs = take(NM)
    f_begin, f_second, f_step = spread(fslot)

    def right(b):
        part = jnp.dot(abuf[...], rbuf[b], preferred_element_type=F32)
        for a in range(NX):
            block = part[a * T:(a + 1) * T]
            to = 4 * a + b
            pbuf[to] = block.astype(BF16)

            @pl.when(to == m)
            def _():
                pown[...] = block

            @pl.when(to != m)
            def _():
                copy(pbuf.at[to], rsbuf.at[m], (d, to), sem_rs + to, sem_rs + m).start()

    rsbuf[m] = jnp.zeros((T, C), BF16)
    a_last()
    own[0].wait()
    own[3].wait()
    right(mine)
    arrived(rbuf.at[yh * 2 + 1 - c], sem_rd)
    right(yh * 2 + 1 - c)
    g_step(2)
    b_first()
    send(bslot(xs[3], c), bslot(xs[3], c), sibling, sem_bd + 1)
    send(bslot(xs[1], c), bslot(xs[1], c), sibling, sem_bd + 2)
    arrived(rbuf.at[other], sem_r)
    send(rbuf.at[other], rbuf.at[other], sibling, sem_rd + 1)
    send(l_in, lbuf.at[mine], across, sem_l)
    right(other)
    arrived(rbuf.at[(1 - yh) * 2 + 1 - c], sem_rd + 1)
    right((1 - yh) * 2 + 1 - c)

    g_step(3)
    b_last()
    send(bslot(xs[2], c), bslot(xs[2], c), sibling, sem_bd + 3)
    own[1].wait()
    for k, xx in enumerate((x, xs[3], xs[1], xs[2])):
        arrived(bslot(xx, 1 - c), sem_bd + k)
    total = jnp.zeros((2 * T, E), F32)
    for j in range(8):
        total = total + jnp.dot(gbuf[j], bbuf[j], preferred_element_type=F32)
    prot[...] = total
    sem_rot, sem_xr = take(), take(3)
    send(prot.at[pl.ds((1 - yh) * T, T)], rprot, across, sem_rot)
    arrived(rprot, sem_rot)
    xrot[pl.ds(x * T, T)] = (prot[pl.ds(yh * T, T)] + rprot[...]).astype(BF16)
    for k in (1, 2, 3):
        send(xrot.at[pl.ds(x * T, T)], xrot.at[pl.ds(x * T, T)], dev(x_=xs[k]), sem_xr + k - 1)

    for src in range(NM):
        pl.when(src != m)(functools.partial(arrived, rsbuf.at[src], sem_rs + src))
    summed = pown[...]
    for src in range(NM):
        summed = summed + rsbuf[src].astype(F32)
    rfull[m] = summed.astype(BF16)
    f_begin()
    f_second()
    f_step(0)

    own[2].wait()
    arrived(lbuf.at[yh * 2 + 1 - c], sem_ld)
    arrived(lbuf.at[other], sem_l)
    send(lbuf.at[other], lbuf.at[other], sibling, sem_ld + 1)
    arrived(lbuf.at[(1 - yh) * 2 + 1 - c], sem_ld + 1)
    for k in (1, 2, 3):
        arrived(xrot.at[pl.ds(xs[4 - k] * T, T)], sem_xr + k - 1)
        arrived(ends.at[xs[4 - k]], sem_e + k - 1)
    f_step(1)
    for b in range(4):
        left[:, b * C:(b + 1) * C] = jnp.dot(xrot[...], lbuf[b], preferred_element_type=F32)
    f_step(2)
    f_step(3)

    slot = lax.broadcasted_iota(jnp.int32, (T, C), 0)
    for a in range(NX):
        stops = [jnp.broadcast_to(ends[a][k:k + 1, :1], (T, C)) for k in range(SEQ_DEV)]
        inside = [(slot < stops[0]) if k == 0 else (slot >= stops[k - 1]) & (slot < stops[k]) for k in range(SEQ_DEV)]
        for b in range(4):
            prod = left[a * T:(a + 1) * T, b * C:(b + 1) * C] * rfull[4 * a + b].astype(F32)
            rows = [jnp.sum(jnp.where(one, prod, 0.0), axis=0, keepdims=True) for one in inside]
            sbuf[4 * a + b] = jnp.concatenate(rows + [jnp.zeros((8 - SEQ_DEV, C), F32)], axis=0)

    sem_s, sem_f = take(NM), take()
    for to in range(NM):
        @pl.when(to != m)
        def _():
            copy(sbuf.at[to], srecv.at[m], (d, to), sem_s + to, sem_s + m).start()
    srecv[m] = sbuf[m]
    for src in range(NM):
        pl.when(src != m)(functools.partial(arrived, srecv.at[src], sem_s + src))
    scores = srecv[0]
    for src in range(1, NM):
        scores = scores + srecv[src]
    column, query = (lax.broadcasted_iota(jnp.int32, (C, 128), k) for k in (0, 1))
    ranks = (column // RANK == query).astype(F32)
    scale = 1.0 / jnp.sqrt(jnp.float32(RANK * TOK_DEV))
    fin_s[...] = jnp.dot(scores, ranks, precision=lax.Precision.HIGHEST, preferred_element_type=F32) * scale
    last = copy(fin_s, fin_r, turn, sem_f)

    @pl.when(turns)
    def _():
        last.start()
        last.wait()

    @pl.when(jnp.logical_not(turns))
    def _():
        fin_r[...] = fin_s[...]

    out[...] = fin_r[:SEQ_DEV, :C // RANK]

    for cp in sent:
        cp.wait_send()
    pl.when(moves)(lambda: move_g.wait_send())
    for to in range(NM):
        @pl.when(to != m)
        def _():
            copy(pbuf.at[to], rsbuf.at[m], (d, to), sem_rs + to, sem_rs + m).wait_send()
            copy(sbuf.at[to], srecv.at[m], (d, to), sem_s + to, sem_s + m).wait_send()
    assert used[0] <= NSEM, used[0]


NSEM = 128


def on_device(out_grads, basis, left_factors, right_factors, activations, spans):
    vmem = pltpu.VMEM
    return pl.pallas_call(
        kernel,
        out_shape=jax.ShapeDtypeStruct((SEQ_DEV, C // RANK), F32),
        in_specs=[pl.BlockSpec(memory_space=pl.ANY)] * 5 + [pl.BlockSpec(memory_space=pltpu.SMEM)],
        out_specs=pl.BlockSpec(memory_space=vmem),
        scratch_shapes=[
            vmem((8, 2 * T, O), BF16),
            vmem((8, O, E), BF16),
            vmem((4, E, C), BF16),
            vmem((4, I, C), BF16),
            vmem((NX * T, I), BF16),
            vmem((2 * T, E), F32),
            vmem((T, E), F32),
            vmem((NX * T, E), BF16),
            vmem((NM, T, C), BF16),
            vmem((T, C), F32),
            vmem((NM, T, C), BF16),
            vmem((NM, T, C), BF16),
            vmem((NX * T, 4 * C), F32),
            vmem((NX, 8, 128), jnp.int32),
            vmem((NM, 8, C), F32),
            vmem((NM, 8, C), F32),
            vmem((8, 128), F32),
            vmem((8, 128), F32),
            pltpu.SemaphoreType.DMA((5,)),
            pltpu.SemaphoreType.DMA((NSEM,)),
            pltpu.SemaphoreType.DMA((NSEM,)),
        ],
        compiler_params=pltpu.CompilerParams(collective_id=0, has_side_effects=True, vmem_limit_bytes=48 << 20),
    )(out_grads, basis, left_factors, right_factors, activations, spans)


def solution(mesh):
    placed = (
        P("dp", "mp"),
        P("dp", "mp"),
        P("mp", "dp"),
        P("mp", "dp"),
        P("dp", "mp"),
        P("dp", None),
    )
    return jax.shard_map(
        on_device, mesh=mesh, in_specs=placed, out_specs=P("dp", "mp"), check_vma=False
    )
```

```python
import functools

import jax
import jax.numpy as jnp
from jax import lax
from jax.experimental import pallas as pl
from jax.experimental.pallas import tpu as pltpu
from jax.sharding import PartitionSpec as P

RANK = 32
TOK_DEV = 128
SEQ_DEV = 4
MESH = pl.DeviceIdType.MESH
BF16, F32 = jnp.bfloat16, jnp.float32

NX, NZ, NM = 4, 8, 16
T, O, E, C, I = 128, 512, 512, 256, 1792


def kernel(g_in, b_in, l_in, r_in, a_in, sp, out, gbuf, bbuf, lbuf, rbuf, abuf, prot, rprot, xrot, pf, pb, yb, zsend, zrecv,
           rfull, left, ends, sbuf, ssend, srecv, fin_s, fin_r, loc, ss, rs):
    d, m = lax.axis_index("dp"), lax.axis_index("mp")
    x, yh, c = d // 4, (d // 2) % 2, d % 2
    yl, z = m // NZ, m % NZ

    def dev(x_=None, yh_=None, c_=None, yl_=None, z_=None):
        pick = lambda new, old: old if new is None else new
        return (4 * pick(x_, x) + 2 * pick(yh_, yh) + pick(c_, c), NZ * pick(yl_, yl) + pick(z_, z))

    xs = [(x + k) % NX for k in range(NX)]
    zr, zl = (z + 1) % NZ, (z + NZ - 1) % NZ
    sibling, across, beside = dev(c_=1 - c), dev(yh_=1 - yh), dev(yl_=1 - yl)
    bit = (m // 2) % 2
    swap_m = m + 2 - 4 * bit
    swapped = (4 * x + 2 * (1 - yh) + c, swap_m)
    turn = (4 * (m // 4) + 2 * yh + c, 4 * x + m % 4)
    turns = x != m // 4

    def greet(to):
        pl.semaphore_signal(pltpu.get_barrier_semaphore(), inc=1, device_id=to, device_id_type=MESH)

    near = [dev(x_=xs[k]) for k in (1, 2, 3)] + [dev(z_=zr), dev(z_=zl), sibling, across, beside, swapped]
    for to in near:
        greet(to)
    pl.semaphore_wait(pltpu.get_barrier_semaphore(), len(near))

    used = [0]

    def take(n=1):
        used[0] += n
        return used[0] - n

    sent = []

    def copy(src, dst, to, sem, sem_there=None):
        sem_there = sem if sem_there is None else sem_there
        return pltpu.make_async_remote_copy(
            src_ref=src, dst_ref=dst, send_sem=ss.at[sem], recv_sem=rs.at[sem_there], device_id=to, device_id_type=MESH
        )

    def send(src, dst, to, sem):
        cp = copy(src, dst, to, sem)
        cp.start()
        sent.append(cp)

    def arrived(dst, sem):
        copy(dst, dst, sibling, sem).wait_recv()

    def gslot(mm, lo=0, n=T):
        return gbuf.at[(mm // 4) * 2 + mm % 2, pl.ds(((mm // 2) % 2) * T + lo, n)]

    def fslot(mm, lo=0, n=T):
        return rfull.at[mm, pl.ds(lo, n)]

    def arow(xx, lo=0, n=T):
        return abuf.at[pl.ds(xx * T + lo, n)]

    def bslot(xx, cc, lo=0, n=O):
        return bbuf.at[xx * 2 + cc, pl.ds(lo, n)]

    def spread(slot):
        sem_pair, sem = take(), take(16)
        half = T // 2

        def at(stream, direction, step):
            return sem + stream * 8 + direction * 4 + step

        def stage(stream, step):
            row = yl if stream == 0 else 1 - yl
            for direction, (to, sign) in enumerate(((zr, -1), (zl, 1))):
                origin = row * NZ + (z + sign * step + NZ) % NZ
                lo, n = (0, T) if step < 3 else (half * direction, half)
                send(slot(origin, lo, n), slot(origin, lo, n), dev(z_=to), at(stream, direction, step))

        def landed(stream, step):
            row = yl if stream == 0 else 1 - yl
            for direction, sign in ((0, -1), (1, 1)):
                origin = row * NZ + (z + sign * (step + 1) + NZ) % NZ
                lo, n = (0, T) if step < 3 else (half * direction, half)
                arrived(slot(origin, lo, n), at(stream, direction, step))

        def begin():
            send(slot(m), slot(m), beside, sem_pair)
            stage(0, 0)

        def second():
            arrived(slot((1 - yl) * NZ + z), sem_pair)
            stage(1, 0)

        def go(stream, k):
            landed(stream, k)
            if k < 3:
                stage(stream, k + 1)

        return begin, second, go

    places = [(a_in, arow(x)), (b_in, bslot(x, c)), (l_in, lbuf.at[yh * 2 + c]), (r_in, rbuf.at[yh * 2 + c])]
    own = [pltpu.make_async_copy(src, dst, loc.at[i]) for i, (src, dst) in enumerate(places)]
    own_g = pltpu.make_async_copy(g_in, gslot(m), loc.at[4])
    sem_g = take()
    move_g = copy(g_in, gslot(swap_m), swapped, sem_g)
    moves = yh != bit
    pl.when(moves)(lambda: move_g.start())
    pl.when(jnp.logical_not(moves))(lambda: own_g.start())

    def ring(src, slot, size, cuts):
        sem = take(2 * len(cuts))
        half = size // 2
        pieces = [(lo, hi - lo) for lo, hi in zip(cuts, cuts[1:])]

        def begin(k):
            lo, n = pieces[k]
            for way, to in ((0, xs[1]), (1, xs[3])):
                send(src.at[pl.ds(lo, n)], slot(x, lo, n), dev(x_=to), sem + 2 * k + way)

        def first():
            for way, to, came in ((0, xs[1], xs[3]), (1, xs[3], xs[1])):
                for k, (lo, n) in enumerate(pieces):
                    arrived(slot(came, lo, n), sem + 2 * k + way)
                send(slot(came, way * half, half), slot(came, way * half, half), dev(x_=to), sem + 2 * len(pieces) + way)

        def last():
            for way in range(2):
                arrived(slot(xs[2], way * half, half), sem + 2 * len(pieces) + way)

        return begin, first, last

    a_begin, a_first, a_last = ring(a_in, arow, T, (0, T))
    b_begin, b_first, b_last = ring(b_in, lambda xx, lo, n: bslot(xx, c, lo, n), O, (0, O // 4, O))
    sem_l, sem_rd, sem_ld, sem_bd = take(), take(2), take(2), take(4)
    sem_r = take(2)
    r_cut = I // 4
    mine, other = yh * 2 + c, (1 - yh) * 2 + c

    def r_rows(slot, k):
        return slot.at[pl.ds(k * r_cut, r_cut + k * (I - 2 * r_cut))]

    def r_send(k):
        send(r_rows(r_in, k), r_rows(rbuf.at[mine], k), across, sem_r + k)

    row = lax.broadcasted_iota(jnp.int32, (8, 128), 0)
    tile = jnp.zeros((8, 128), jnp.int32)
    end = 0
    for k in range(SEQ_DEV):
        end = end + sp[0, k]
        tile = jnp.where(row == k, end, tile)
    ends[x] = tile
    sem_e = take(3)
    for k in (1, 2, 3):
        send(ends.at[x], ends.at[x], dev(x_=xs[k]), sem_e + k - 1)
    a_begin(0)
    b_begin(0)
    r_send(0)
    send(r_in, rbuf.at[mine], sibling, sem_rd)
    send(b_in, bslot(x, c), sibling, sem_bd)
    send(l_in, lbuf.at[mine], sibling, sem_ld)
    for cp in own:
        cp.start()

    pl.when(moves)(lambda: copy(g_in, gslot(m), swapped, sem_g).wait_recv())
    pl.when(jnp.logical_not(moves))(lambda: own_g.wait())
    g_begin, g_second, g_go = spread(gslot)
    g_begin()
    r_send(1)
    g_second()
    g_go(0, 0)
    a_first()
    b_begin(1)
    g_go(1, 0)
    g_go(0, 1)

    def right(b):
        part = jnp.dot(abuf[...], rbuf[b], preferred_element_type=F32)
        for a in range(NX):
            pf[4 * a + b] = part[a * T:(a + 1) * T]

    sem_y = take(NZ)

    def pair_sum(b):
        for zz in (b, b + 4):
            pb[zz] = pf[(1 - yl) * NZ + zz].astype(BF16)
            send(pb.at[zz], yb.at[zz], beside, sem_y + zz)

    a_last()
    own[0].wait()
    own[3].wait()
    g_go(1, 1)
    right(mine)
    arrived(rbuf.at[yh * 2 + 1 - c], sem_rd)
    g_go(0, 2)
    right(yh * 2 + 1 - c)
    g_go(1, 2)
    pair_sum(mine)
    pair_sum(yh * 2 + 1 - c)
    for k in range(2):
        arrived(r_rows(rbuf.at[other], k), sem_r + k)
    send(rbuf.at[other], rbuf.at[other], sibling, sem_rd + 1)
    right(other)
    pair_sum(other)
    b_first()
    send(bslot(xs[3], c), bslot(xs[3], c), sibling, sem_bd + 1)
    send(bslot(xs[1], c), bslot(xs[1], c), sibling, sem_bd + 2)
    arrived(rbuf.at[(1 - yh) * 2 + 1 - c], sem_rd + 1)
    right((1 - yh) * 2 + 1 - c)
    pair_sum((1 - yh) * 2 + 1 - c)
    send(l_in, lbuf.at[mine], across, sem_l)
    g_go(0, 3)
    g_go(1, 3)

    zs = [(z + k) % NZ for k in (4, 3, 5, 2, 6, 1, 7, 0)]

    def both(k):
        arrived(yb.at[zs[k]], sem_y + zs[k])

    def partial(k, u):
        cols = pl.ds(u * (C // 2), C // 2)
        return pf[yl * NZ + zs[k], :, cols] + yb[zs[k], :, cols].astype(F32)

    sem_z = take(16)
    half = T // 2

    def hop(way, step, u):
        return sem_z + way * 8 + step * 2 + u

    def z_first():
        both(0)
        for u in range(2):
            chunk = partial(0, u)
            for way, to in enumerate((zr, zl)):
                zsend[way, 0, u, :half] = chunk[way * half:(way + 1) * half]
                send(zsend.at[way, 0, u, pl.ds(0, half)], zrecv.at[way, 0, u, pl.ds(0, half)], dev(z_=to), hop(way, 0, u))

    def z_next(step):
        for way in range(2):
            both(2 * step - 1 + way)
        for u in range(2):
            for way, to in enumerate((zr, zl)):
                n = half if step == 1 else T
                arrived(zrecv.at[way, step - 1, u, pl.ds(0, n)], hop(way, step - 1, u))
                chunk = partial(2 * step - 1 + way, u)
                if step == 1:
                    zsend[way, step, u] = chunk
                    rows = pl.ds(way * half, half)
                    zsend[way, step, u, rows] = zsend[way, step, u, rows] + zrecv[way, 0, u, :half]
                else:
                    zsend[way, step, u] = chunk + zrecv[way, step - 1, u]
                send(zsend.at[way, step, u], zrecv.at[way, step, u], dev(z_=to), hop(way, step, u))

    z_first()
    b_last()
    send(bslot(xs[2], c), bslot(xs[2], c), sibling, sem_bd + 3)
    z_next(1)

    own[1].wait()
    for k, xx in enumerate((x, xs[3], xs[1], xs[2])):
        arrived(bslot(xx, 1 - c), sem_bd + k)
    total = jnp.zeros((2 * T, E), F32)
    for j in range(8):
        total = total + jnp.dot(gbuf[j], bbuf[j], preferred_element_type=F32)
    prot[...] = total
    sem_rot, sem_xr = take(), take(3)
    send(prot.at[pl.ds((1 - yh) * T, T)], rprot, across, sem_rot)
    z_next(2)
    z_next(3)
    arrived(rprot, sem_rot)
    xrot[pl.ds(x * T, T)] = (prot[pl.ds(yh * T, T)] + rprot[...]).astype(BF16)
    for k in (1, 2, 3):
        send(xrot.at[pl.ds(x * T, T)], xrot.at[pl.ds(x * T, T)], dev(x_=xs[k]), sem_xr + k - 1)

    slot = lax.broadcasted_iota(jnp.int32, (T, C), 0)

    def product(mm):
        prod = left[mm] * rfull[mm].astype(F32)
        stops = ends[mm // 4]
        below = [slot < jnp.broadcast_to(stops[k:k + 1, :1], (T, C)) for k in range(SEQ_DEV)]
        rows = []
        for k in range(SEQ_DEV):
            inside = below[0] if k == 0 else below[k] & jnp.logical_not(below[k - 1])
            rows.append(jnp.sum(jnp.where(inside, prod, 0.0), axis=0, keepdims=True))
        sbuf[pl.ds(pl.multiple_of(mm * 8, 8), 8)] = jnp.concatenate(rows + [jnp.zeros((8 - SEQ_DEV, C), F32)], axis=0)

    both(7)
    for u in range(2):
        total = partial(7, u)
        for way in range(2):
            arrived(zrecv.at[way, 3, u], hop(way, 3, u))
            total = total + zrecv[way, 3, u]
        rfull[m, :, u * (C // 2):(u + 1) * (C // 2)] = total.astype(BF16)
    f_begin, f_second, f_go = spread(fslot)
    f_begin()
    f_second()
    f_go(0, 0)
    f_go(1, 0)
    own[2].wait()
    arrived(lbuf.at[yh * 2 + 1 - c], sem_ld)
    arrived(lbuf.at[other], sem_l)
    send(lbuf.at[other], lbuf.at[other], sibling, sem_ld + 1)
    arrived(lbuf.at[(1 - yh) * 2 + 1 - c], sem_ld + 1)
    for k in (1, 2, 3):
        arrived(xrot.at[pl.ds(xs[4 - k] * T, T)], sem_xr + k - 1)
        arrived(ends.at[xs[4 - k]], sem_e + k - 1)
    for b in range(4):
        part = jnp.dot(xrot[...], lbuf[b], preferred_element_type=F32)
        for a in range(NX):
            left[4 * a + b] = part[a * T:(a + 1) * T]
    f_go(0, 1)
    f_go(1, 1)
    product(m)
    product((1 - yl) * NZ + z)
    for k in range(4):
        for stream in range(2):
            if k >= 2:
                f_go(stream, k)
            for far in ((k + 1, NZ - 1 - k) if k < 3 else (4,)):
                product((yl if stream == 0 else 1 - yl) * NZ + (z + far) % NZ)

    sem_s, sem_f = take(NM), take()
    column, query = (lax.broadcasted_iota(jnp.int32, (C, 128), k) for k in (0, 1))
    ranks = (column // RANK == query).astype(F32)
    tiles = jnp.dot(sbuf[...], ranks, precision=lax.Precision.HIGHEST, preferred_element_type=F32)
    for to in range(NM):
        ssend[to] = tiles[to * 8:(to + 1) * 8]

        @pl.when(to != m)
        def _():
            copy(ssend.at[to], srecv.at[m], (d, to), sem_s + to, sem_s + m).start()
    srecv[m] = ssend[m]
    for src in range(NM):
        pl.when(src != m)(functools.partial(arrived, srecv.at[src], sem_s + src))
    scores = srecv[0]
    for src in range(1, NM):
        scores = scores + srecv[src]
    fin_s[...] = scores * (1.0 / jnp.sqrt(jnp.float32(RANK * TOK_DEV)))
    last = copy(fin_s, fin_r, turn, sem_f)

    @pl.when(turns)
    def _():
        last.start()
        last.wait()

    @pl.when(jnp.logical_not(turns))
    def _():
        fin_r[...] = fin_s[...]

    out[...] = fin_r[:SEQ_DEV, :C // RANK]

    for cp in sent:
        cp.wait_send()
    pl.when(moves)(lambda: move_g.wait_send())
    for to in range(NM):
        @pl.when(to != m)
        def _():
            copy(ssend.at[to], srecv.at[m], (d, to), sem_s + to, sem_s + m).wait_send()
    assert used[0] <= NSEM, used[0]


NSEM = 160


def on_device(out_grads, basis, left_factors, right_factors, activations, spans):
    vmem = pltpu.VMEM
    return pl.pallas_call(
        kernel,
        out_shape=jax.ShapeDtypeStruct((SEQ_DEV, C // RANK), F32),
        in_specs=[pl.BlockSpec(memory_space=pltpu.HBM)] * 5 + [pl.BlockSpec(memory_space=pltpu.SMEM)],
        out_specs=pl.BlockSpec(memory_space=vmem),
        scratch_shapes=[
            vmem((8, 2 * T, O), BF16),
            vmem((8, O, E), BF16),
            vmem((4, E, C), BF16),
            vmem((4, I, C), BF16),
            vmem((NX * T, I), BF16),
            vmem((2 * T, E), F32),
            vmem((T, E), F32),
            vmem((NX * T, E), BF16),
            vmem((NM, T, C), F32),
            vmem((NZ, T, C), BF16),
            vmem((NZ, T, C), BF16),
            vmem((2, 4, 2, T, C // 2), F32),
            vmem((2, 4, 2, T, C // 2), F32),
            vmem((NM, T, C), BF16),
            vmem((NM, T, C), F32),
            vmem((NX, 8, 128), jnp.int32),
            vmem((NM * 8, C), F32),
            vmem((NM, 8, 128), F32),
            vmem((NM, 8, 128), F32),
            vmem((8, 128), F32),
            vmem((8, 128), F32),
            pltpu.SemaphoreType.DMA((5,)),
            pltpu.SemaphoreType.DMA((NSEM,)),
            pltpu.SemaphoreType.DMA((NSEM,)),
        ],
        compiler_params=pltpu.CompilerParams(collective_id=0, has_side_effects=True, vmem_limit_bytes=60 << 20),
    )(out_grads, basis, left_factors, right_factors, activations, spans)


def solution(mesh):
    placed = (
        P("dp", "mp"),
        P("dp", "mp"),
        P("mp", "dp"),
        P("mp", "dp"),
        P("dp", "mp"),
        P("dp", None),
    )
    return jax.shard_map(
        on_device, mesh=mesh, in_specs=placed, out_specs=P("dp", "mp"), check_vma=False
    )
```

```python
import functools

import jax
import jax.numpy as jnp
from jax import lax
from jax.experimental import pallas as pl
from jax.experimental.pallas import tpu as pltpu
from jax.sharding import PartitionSpec as P

RANK = 32
TOK_DEV = 128
SEQ_DEV = 4
MESH = pl.DeviceIdType.MESH
BF16, F32 = jnp.bfloat16, jnp.float32

NX, NZ, NM = 4, 8, 16
T, O, E, C, I = 128, 512, 512, 256, 1792
H = T // 2


def kernel(g_in, b_in, l_in, r_in, a_in, sp, out, gbuf, bbuf, lbuf, rbuf, abuf, prot, rprot, xrot, pf, pb, yb, zsend, zrecv,
           rfull, left, ends, sbuf, ssend, srecv, loc, ss, rs):
    d, m = lax.axis_index("dp"), lax.axis_index("mp")
    x, yh, c = d // 4, (d // 2) % 2, d % 2
    yl, z = m // NZ, m % NZ

    def dev(x_=None, yh_=None, c_=None, yl_=None, z_=None):
        pick = lambda new, old: old if new is None else new
        return (4 * pick(x_, x) + 2 * pick(yh_, yh) + pick(c_, c), NZ * pick(yl_, yl) + pick(z_, z))

    xs = [(x + k) % NX for k in range(NX)]
    zr, zl = (z + 1) % NZ, (z + NZ - 1) % NZ
    sibling, across, beside = dev(c_=1 - c), dev(yh_=1 - yh), dev(yl_=1 - yl)
    bit = (m // 2) % 2
    swap_m = m + 2 - 4 * bit
    swapped = (4 * x + 2 * (1 - yh) + c, swap_m)

    def greet(to):
        pl.semaphore_signal(pltpu.get_barrier_semaphore(), inc=1, device_id=to, device_id_type=MESH)

    near = [dev(x_=xs[k]) for k in (1, 2, 3)] + [dev(z_=zr), dev(z_=zl), sibling, across, beside, swapped]
    for to in near:
        greet(to)
    pl.semaphore_wait(pltpu.get_barrier_semaphore(), len(near))

    used = [0]

    def take(n=1):
        used[0] += n
        return used[0] - n

    sent = []

    def copy(src, dst, to, sem, sem_there=None):
        sem_there = sem if sem_there is None else sem_there
        return pltpu.make_async_remote_copy(
            src_ref=src, dst_ref=dst, send_sem=ss.at[sem], recv_sem=rs.at[sem_there], device_id=to, device_id_type=MESH
        )

    def send(src, dst, to, sem):
        cp = copy(src, dst, to, sem)
        cp.start()
        sent.append(cp)

    def arrived(dst, sem):
        copy(dst, dst, sibling, sem).wait_recv()

    def gslot(mm, lo=0, n=T):
        return gbuf.at[(mm // 4) * 2 + mm % 2, pl.ds(((mm // 2) % 2) * T + lo, n)]

    def fslot(u):
        return lambda mm, lo=0, n=H: rfull.at[u, mm % NZ, pl.ds((mm // NZ) * H + lo, n)]

    def arow(xx, lo=0, n=T):
        return abuf.at[pl.ds(xx * T + lo, n)]

    def bslot(xx, cc, lo=0, n=O):
        return bbuf.at[xx * 2 + cc, pl.ds(lo, n)]

    def spread(slot, rows):
        sem_pair, sem = take(), take(16)
        half = rows // 2

        def at(stream, direction, step):
            return sem + stream * 8 + direction * 4 + step

        def stage(stream, step):
            row = yl if stream == 0 else 1 - yl
            for direction, (to, sign) in enumerate(((zr, -1), (zl, 1))):
                origin = row * NZ + (z + sign * step + NZ) % NZ
                lo, n = (0, rows) if step < 3 else (half * direction, half)
                send(slot(origin, lo, n), slot(origin, lo, n), dev(z_=to), at(stream, direction, step))

        def landed(stream, step):
            row = yl if stream == 0 else 1 - yl
            for direction, sign in ((0, -1), (1, 1)):
                origin = row * NZ + (z + sign * (step + 1) + NZ) % NZ
                lo, n = (0, rows) if step < 3 else (half * direction, half)
                arrived(slot(origin, lo, n), at(stream, direction, step))

        def begin():
            send(slot(m), slot(m), beside, sem_pair)
            stage(0, 0)

        def second():
            arrived(slot((1 - yl) * NZ + z), sem_pair)
            stage(1, 0)

        def go(stream, k):
            landed(stream, k)
            if k < 3:
                stage(stream, k + 1)

        return begin, second, go

    def relay(slot, rows):
        sem, half = take(17), rows // 2

        def piece(row, direction, step):
            origin = row * NZ + (z + (-step, step)[direction] + NZ) % NZ
            return slot(origin, 0, rows) if step < 4 else slot(origin, half * direction, half)

        def begin():
            for direction, to in enumerate((zr, zl)):
                send(slot(m), slot(m), dev(z_=to), sem + direction)
            send(slot(m), slot(m), beside, sem + 16)

        def go(k):
            for direction, to in enumerate((zr, zl)):
                block = piece(yl, direction, k + 1)
                arrived(block, sem + 2 * k + direction)
                if k < 3:
                    onward = block if k < 2 else slot(yl * NZ + (z + (-3, 3)[direction] + NZ) % NZ, half * direction, half)
                    send(onward, onward, dev(z_=to), sem + 2 * (k + 1) + direction)
                send(block, block, beside, sem + 8 + 2 * k + direction)

        def pair(k):
            if k < 0:
                arrived(slot((1 - yl) * NZ + z), sem + 16)
            else:
                for direction in range(2):
                    arrived(piece(1 - yl, direction, k + 1), sem + 8 + 2 * k + direction)

        return begin, go, pair

    places = [(a_in, arow(x)), (b_in, bslot(x, c)), (l_in, lbuf.at[yh * 2 + c]), (r_in, rbuf.at[yh * 2 + c])]
    own = [pltpu.make_async_copy(src, dst, loc.at[i]) for i, (src, dst) in enumerate(places)]
    own_g = pltpu.make_async_copy(g_in, gslot(m), loc.at[4])
    sem_g = take()
    move_g = copy(g_in, gslot(swap_m), swapped, sem_g)
    moves = yh != bit
    pl.when(moves)(lambda: move_g.start())
    pl.when(jnp.logical_not(moves))(lambda: own_g.start())

    def ring(src, slot, size, cuts):
        sem = take(2 * len(cuts))
        half = size // 2
        pieces = [(lo, hi - lo) for lo, hi in zip(cuts, cuts[1:])]

        def begin(k):
            lo, n = pieces[k]
            for way, to in ((0, xs[1]), (1, xs[3])):
                send(src.at[pl.ds(lo, n)], slot(x, lo, n), dev(x_=to), sem + 2 * k + way)

        def first():
            for way, to, came in ((0, xs[1], xs[3]), (1, xs[3], xs[1])):
                for k, (lo, n) in enumerate(pieces):
                    arrived(slot(came, lo, n), sem + 2 * k + way)
                send(slot(came, way * half, half), slot(came, way * half, half), dev(x_=to), sem + 2 * len(pieces) + way)

        def last():
            for way in range(2):
                arrived(slot(xs[2], way * half, half), sem + 2 * len(pieces) + way)

        return begin, first, last

    a_begin, a_first, a_last = ring(a_in, arow, T, (0, T))
    b_begin, b_first, b_last = ring(b_in, lambda xx, lo, n: bslot(xx, c, lo, n), O, (0, O // 4, O))
    sem_l, sem_rd, sem_ld, sem_bd = take(), take(2), take(2), take(4)
    sem_r = take(2)
    r_cut = I // 4
    mine, other = yh * 2 + c, (1 - yh) * 2 + c

    def r_rows(slot, k):
        return slot.at[pl.ds(k * r_cut, r_cut + k * (I - 2 * r_cut))]

    def r_send(k):
        send(r_rows(r_in, k), r_rows(rbuf.at[mine], k), across, sem_r + k)

    row = lax.broadcasted_iota(jnp.int32, (8, 128), 0)
    tile = jnp.zeros((8, 128), jnp.int32)
    end = 0
    for k in range(SEQ_DEV):
        end = end + sp[0, k]
        tile = jnp.where(row == k, end, tile)
    ends[x] = tile
    sem_e = take(3)
    for k in (1, 2, 3):
        send(ends.at[x], ends.at[x], dev(x_=xs[k]), sem_e + k - 1)
    a_begin(0)
    b_begin(0)
    r_send(0)
    send(r_in, rbuf.at[mine], sibling, sem_rd)
    send(b_in, bslot(x, c), sibling, sem_bd)
    send(l_in, lbuf.at[mine], sibling, sem_ld)
    for cp in own:
        cp.start()

    pl.when(moves)(lambda: copy(g_in, gslot(m), swapped, sem_g).wait_recv())
    pl.when(jnp.logical_not(moves))(lambda: own_g.wait())
    g_begin, g_second, g_go = spread(gslot, T)
    g_begin()
    r_send(1)
    g_go(0, 0)
    g_second()
    a_first()
    b_begin(1)
    g_go(0, 1)
    g_go(1, 0)

    def right(u, cc):
        part = jnp.dot(abuf[...], rbuf[(mine // 2 if u == 0 else other // 2) * 2 + cc], preferred_element_type=F32)
        for a in range(NX):
            pf[u, 2 * a + cc] = part[a * T:(a + 1) * T]

    zs = [(z + k) % NZ for k in (4, 3, 5, 2, 6, 1, 7, 0)]
    sem_y, sem_z = take(4), take(16)
    quarter = H // 2
    keep, give = pl.ds(yl * H, H), pl.ds((1 - yl) * H, H)

    lots = ((0, 3), (3, 5))
    met = set()

    def pair_sum(u):
        for k, zz in enumerate(zs):
            pb[u, k] = pf[u, zz, give].astype(BF16)
            for lot, (first, n) in enumerate(lots):
                if k == first + n - 1:
                    blocks = pl.ds(first, n)
                    send(pb.at[u, blocks], yb.at[u, blocks], beside, sem_y + 2 * u + lot)

    def partial(u, k):
        lot = 0 if k < lots[1][0] else 1
        if (u, lot) not in met:
            met.add((u, lot))
            arrived(yb.at[u, pl.ds(*lots[lot])], sem_y + 2 * u + lot)
        return pf[u, zs[k], keep] + yb[u, k].astype(F32)

    def hop(u, way, step):
        return sem_z + 8 * u + way * 4 + step

    def z_first(u):
        chunk = partial(u, 0)
        for way, to in enumerate((zr, zl)):
            zsend[u, way, 0, :quarter] = chunk[way * quarter:(way + 1) * quarter]
            send(zsend.at[u, way, 0, pl.ds(0, quarter)], zrecv.at[u, way, 0, pl.ds(0, quarter)], dev(z_=to), hop(u, way, 0))

    def z_next(u, step):
        for way, to in enumerate((zr, zl)):
            chunk = partial(u, 2 * step - 1 + way)
            arrived(zrecv.at[u, way, step - 1, pl.ds(0, quarter if step == 1 else H)], hop(u, way, step - 1))
            if step == 1:
                zsend[u, way, step] = chunk
                rows = pl.ds(way * quarter, quarter)
                zsend[u, way, step, rows] = zsend[u, way, step, rows] + zrecv[u, way, 0, :quarter]
            else:
                zsend[u, way, step] = chunk + zrecv[u, way, step - 1]
            send(zsend.at[u, way, step], zrecv.at[u, way, step], dev(z_=to), hop(u, way, step))

    def z_last(u):
        total = partial(u, 7)
        for way in range(2):
            arrived(zrecv.at[u, way, 3], hop(u, way, 3))
            total = total + zrecv[u, way, 3]
        rfull[u, z, keep] = total.astype(BF16)

    a_last()
    own[0].wait()
    own[3].wait()
    g_go(0, 2)
    right(0, c)
    arrived(rbuf.at[yh * 2 + 1 - c], sem_rd)
    right(0, 1 - c)
    pair_sum(0)
    g_go(1, 1)
    for k in range(2):
        arrived(r_rows(rbuf.at[other], k), sem_r + k)
    send(rbuf.at[other], rbuf.at[other], sibling, sem_rd + 1)
    right(1, c)
    z_first(0)
    arrived(rbuf.at[(1 - yh) * 2 + 1 - c], sem_rd + 1)
    right(1, 1 - c)
    pair_sum(1)
    send(l_in, lbuf.at[mine], across, sem_l)
    g_go(1, 2)
    z_next(0, 1)
    b_first()
    send(bslot(xs[3], c), bslot(xs[3], c), sibling, sem_bd + 1)
    send(bslot(xs[1], c), bslot(xs[1], c), sibling, sem_bd + 2)
    g_go(0, 3)
    z_next(0, 2)
    z_first(1)
    g_go(1, 3)
    z_next(0, 3)
    z_next(1, 1)
    b_last()
    send(bslot(xs[2], c), bslot(xs[2], c), sibling, sem_bd + 3)

    own[1].wait()
    for k, xx in enumerate((x, xs[3], xs[1], xs[2])):
        arrived(bslot(xx, 1 - c), sem_bd + k)
    total = jnp.zeros((2 * T, E), F32)
    for j in range(8):
        total = total + jnp.dot(gbuf[j], bbuf[j], preferred_element_type=F32)
    prot[...] = total
    sem_rot, sem_xr = take(), take(3)
    send(prot.at[pl.ds((1 - yh) * T, T)], rprot, across, sem_rot)
    f0_begin, f0_go, f0_pair = relay(fslot(0), H)
    f1_begin, f1_go, f1_pair = relay(fslot(1), H)
    z_next(1, 2)
    z_last(0)
    f0_begin()
    z_next(1, 3)
    f0_go(0)
    arrived(lbuf.at[other], sem_l)
    send(lbuf.at[other], lbuf.at[other], sibling, sem_ld + 1)
    z_last(1)
    f1_begin()
    arrived(rprot, sem_rot)
    xrot[pl.ds(x * T, T)] = (prot[pl.ds(yh * T, T)] + rprot[...]).astype(BF16)
    for k in (1, 2, 3):
        send(xrot.at[pl.ds(x * T, T)], xrot.at[pl.ds(x * T, T)], dev(x_=xs[k]), sem_xr + k - 1)
    f0_go(1)
    f1_go(0)
    f0_go(2)
    f1_go(1)
    f0_go(3)
    f1_go(2)

    own[2].wait()
    arrived(lbuf.at[yh * 2 + 1 - c], sem_ld)
    arrived(lbuf.at[(1 - yh) * 2 + 1 - c], sem_ld + 1)
    for k in (1, 2, 3):
        arrived(xrot.at[pl.ds(xs[4 - k] * T, T)], sem_xr + k - 1)
        arrived(ends.at[xs[4 - k]], sem_e + k - 1)
    f1_go(3)
    for u in range(2):
        for cc in range(2):
            slot_of = (mine // 2 if u == 0 else other // 2) * 2 + cc
            part = jnp.dot(xrot[...], lbuf[slot_of], preferred_element_type=F32)
            for a in range(NX):
                left[u, 2 * a + cc] = part[a * T:(a + 1) * T]

    token = lax.broadcasted_iota(jnp.int32, (T, C), 0)

    def product(u, zz):
        prod = left[u, zz] * rfull[u, zz].astype(F32)
        stops = ends[zz // 2]
        below = [token < jnp.broadcast_to(stops[k:k + 1, :1], (T, C)) for k in range(SEQ_DEV)]
        rows = []
        for k in range(SEQ_DEV):
            inside = below[0] if k == 0 else below[k] & jnp.logical_not(below[k - 1])
            rows.append(jnp.sum(jnp.where(inside, prod, 0.0), axis=0, keepdims=True))
        at = (u * NZ + zz) * 8
        sbuf[pl.ds(pl.multiple_of(at, 8), 8)] = jnp.concatenate(rows + [jnp.zeros((8 - SEQ_DEV, C), F32)], axis=0)

    for k in range(-1, 4):
        for u, pair in enumerate((f0_pair, f1_pair)):
            pair(k)
            for far in {-1: (0,), 3: (4,)}.get(k, (k + 1, NZ - 1 - k)):
                product(u, (z + far) % NZ)

    sem_s = take(NM)
    column, query = (lax.broadcasted_iota(jnp.int32, (C, 128), k) for k in (0, 1))
    ranks = (column // RANK == query).astype(F32)
    tiles = jnp.dot(sbuf[...], ranks, precision=lax.Precision.HIGHEST, preferred_element_type=F32)
    finals = []
    for u in range(2):
        for zz in range(NZ):
            n = u * NZ + zz
            ssend[n] = tiles[n * 8:(n + 1) * 8]
            to_d, to_m = 4 * (zz // 2) + 2 * yh + c, 4 * x + (mine // 2 if u == 0 else other // 2) * 2 + zz % 2
            here = (to_d == d) & (to_m == m)
            cp = copy(ssend.at[n], srecv.at[m], (to_d, to_m), sem_s + n, sem_s + m)
            finals.append((here, cp))
            pl.when(jnp.logical_not(here))(cp.start)

            @pl.when(here)
            def _():
                srecv[m] = ssend[n]

    for src in range(NM):
        pl.when(jnp.logical_not((x == m // 4) & (m == src)))(functools.partial(arrived, srecv.at[src], sem_s + src))
    scores = srecv[0]
    for src in range(1, NM):
        scores = scores + srecv[src]
    scores = scores * (1.0 / jnp.sqrt(jnp.float32(RANK * TOK_DEV)))
    out[...] = scores[:SEQ_DEV, :C // RANK]

    for cp in sent:
        cp.wait_send()
    pl.when(moves)(lambda: move_g.wait_send())
    for here, cp in finals:
        pl.when(jnp.logical_not(here))(cp.wait_send)
    assert used[0] <= NSEM, used[0]


NSEM = 160


def on_device(out_grads, basis, left_factors, right_factors, activations, spans):
    vmem = pltpu.VMEM
    return pl.pallas_call(
        kernel,
        out_shape=jax.ShapeDtypeStruct((SEQ_DEV, C // RANK), F32),
        in_specs=[pl.BlockSpec(memory_space=pltpu.HBM)] * 5 + [pl.BlockSpec(memory_space=pltpu.SMEM)],
        out_specs=pl.BlockSpec(memory_space=vmem),
        scratch_shapes=[
            vmem((8, 2 * T, O), BF16),
            vmem((8, O, E), BF16),
            vmem((4, E, C), BF16),
            vmem((4, I, C), BF16),
            vmem((NX * T, I), BF16),
            vmem((2 * T, E), F32),
            vmem((T, E), F32),
            vmem((NX * T, E), BF16),
            vmem((2, NZ, T, C), F32),
            vmem((2, NZ, H, C), BF16),
            vmem((2, NZ, H, C), BF16),
            vmem((2, 2, 4, H, C), F32),
            vmem((2, 2, 4, H, C), F32),
            vmem((2, NZ, T, C), BF16),
            vmem((2, NZ, T, C), F32),
            vmem((NX, 8, 128), jnp.int32),
            vmem((NM * 8, C), F32),
            vmem((NM, 8, 128), F32),
            vmem((NM, 8, 128), F32),
            pltpu.SemaphoreType.DMA((5,)),
            pltpu.SemaphoreType.DMA((NSEM,)),
            pltpu.SemaphoreType.DMA((NSEM,)),
        ],
        compiler_params=pltpu.CompilerParams(collective_id=0, has_side_effects=True, vmem_limit_bytes=60 << 20),
    )(out_grads, basis, left_factors, right_factors, activations, spans)


def solution(mesh):
    placed = (
        P("dp", "mp"),
        P("dp", "mp"),
        P("mp", "dp"),
        P("mp", "dp"),
        P("dp", "mp"),
        P("dp", None),
    )
    return jax.shard_map(
        on_device, mesh=mesh, in_specs=placed, out_specs=P("dp", "mp"), check_vma=False
    )
```

```python
import functools

import jax
import jax.numpy as jnp
from jax import lax
from jax.experimental import pallas as pl
from jax.experimental.pallas import tpu as pltpu
from jax.sharding import PartitionSpec as P

RANK = 32
TOK_DEV = 128
SEQ_DEV = 4
MESH = pl.DeviceIdType.MESH
BF16, F32 = jnp.bfloat16, jnp.float32

NX, NZ, NM = 4, 8, 16
T, O, E, C, I = 128, 512, 512, 256, 1792
H = T // 2


def kernel(g_in, b_in, l_in, r_in, a_in, sp, out, gbuf, bbuf, lbuf, rbuf, abuf, prot, rprot, xrot, pf, pb, yb, zsend, zrecv,
           rfull, left, ends, sbuf, ssend, srecv, loc, ss, rs):
    d, m = lax.axis_index("dp"), lax.axis_index("mp")
    x, yh, c = d // 4, (d // 2) % 2, d % 2
    yl, z = m // NZ, m % NZ

    def dev(x_=None, yh_=None, c_=None, yl_=None, z_=None):
        pick = lambda new, old: old if new is None else new
        return (4 * pick(x_, x) + 2 * pick(yh_, yh) + pick(c_, c), NZ * pick(yl_, yl) + pick(z_, z))

    xs = [(x + k) % NX for k in range(NX)]
    zr, zl = (z + 1) % NZ, (z + NZ - 1) % NZ
    sibling, across, beside = dev(c_=1 - c), dev(yh_=1 - yh), dev(yl_=1 - yl)
    bit = (m // 2) % 2
    swap_m = m + 2 - 4 * bit
    swapped = (4 * x + 2 * (1 - yh) + c, swap_m)

    def greet(to):
        pl.semaphore_signal(pltpu.get_barrier_semaphore(), inc=1, device_id=to, device_id_type=MESH)

    near = [dev(x_=xs[k]) for k in (1, 2, 3)] + [dev(z_=zr), dev(z_=zl), sibling, across, beside, swapped]
    for to in near:
        greet(to)
    pl.semaphore_wait(pltpu.get_barrier_semaphore(), len(near))

    used = [0]

    def take(n=1):
        used[0] += n
        return used[0] - n

    sent = []

    def copy(src, dst, to, sem, sem_there=None):
        sem_there = sem if sem_there is None else sem_there
        return pltpu.make_async_remote_copy(
            src_ref=src, dst_ref=dst, send_sem=ss.at[sem], recv_sem=rs.at[sem_there], device_id=to, device_id_type=MESH
        )

    def send(src, dst, to, sem):
        cp = copy(src, dst, to, sem)
        cp.start()
        sent.append(cp)

    def arrived(dst, sem):
        copy(dst, dst, sibling, sem).wait_recv()

    def gslot(mm, lo=0, n=T):
        return gbuf.at[(mm // 4) * 2 + mm % 2, pl.ds(((mm // 2) % 2) * T + lo, n)]

    def fslot(u):
        return lambda mm, lo=0, n=H: rfull.at[u, mm % NZ, pl.ds((mm // NZ) * H + lo, n)]

    def arow(xx, lo=0, n=T):
        return abuf.at[pl.ds(xx * T + lo, n)]

    def bslot(xx, cc, lo=0, n=O):
        return bbuf.at[xx * 2 + cc, pl.ds(lo, n)]

    def spread(slot, rows):
        sem_pair, sem = take(), take(16)
        half = rows // 2

        def at(stream, direction, step):
            return sem + stream * 8 + direction * 4 + step

        def stage(stream, step):
            row = yl if stream == 0 else 1 - yl
            for direction, (to, sign) in enumerate(((zr, -1), (zl, 1))):
                origin = row * NZ + (z + sign * step + NZ) % NZ
                lo, n = (0, rows) if step < 3 else (half * direction, half)
                send(slot(origin, lo, n), slot(origin, lo, n), dev(z_=to), at(stream, direction, step))

        def landed(stream, step):
            row = yl if stream == 0 else 1 - yl
            for direction, sign in ((0, -1), (1, 1)):
                origin = row * NZ + (z + sign * (step + 1) + NZ) % NZ
                lo, n = (0, rows) if step < 3 else (half * direction, half)
                arrived(slot(origin, lo, n), at(stream, direction, step))

        def begin():
            send(slot(m), slot(m), beside, sem_pair)
            stage(0, 0)

        def second():
            arrived(slot((1 - yl) * NZ + z), sem_pair)
            stage(1, 0)

        def go(stream, k):
            landed(stream, k)
            if k < 3:
                stage(stream, k + 1)

        return begin, second, go

    def relay(slot, rows):
        sem, half = take(17), rows // 2

        def piece(row, direction, step):
            origin = row * NZ + (z + (-step, step)[direction] + NZ) % NZ
            return slot(origin, 0, rows) if step < 4 else slot(origin, half * direction, half)

        def begin():
            for far in (1, 2):
                for direction in range(2):
                    to = dev(z_=(z + (far, NZ - far)[direction]) % NZ)
                    send(slot(m), slot(m), to, sem + 2 * (far - 1) + direction)
            send(slot(m), slot(m), beside, sem + 16)

        def go(k):
            for direction in range(2):
                block = piece(yl, direction, k + 1)
                arrived(block, sem + 2 * k + direction)
                if k == 1:
                    send(block, block, dev(z_=(zr, zl)[direction]), sem + 4 + direction)
                    part = slot(yl * NZ + (z + (-2, 2)[direction] + NZ) % NZ, half * direction, half)
                    send(part, part, dev(z_=(z + (2, NZ - 2)[direction]) % NZ), sem + 6 + direction)
                send(block, block, beside, sem + 8 + 2 * k + direction)

        def pair(k):
            if k < 0:
                arrived(slot((1 - yl) * NZ + z), sem + 16)
            else:
                for direction in range(2):
                    arrived(piece(1 - yl, direction, k + 1), sem + 8 + 2 * k + direction)

        return begin, go, pair

    places = [(a_in, arow(x)), (b_in, bslot(x, c)), (l_in, lbuf.at[yh * 2 + c]), (r_in, rbuf.at[yh * 2 + c])]
    own = [pltpu.make_async_copy(src, dst, loc.at[i]) for i, (src, dst) in enumerate(places)]
    own_g = pltpu.make_async_copy(g_in, gslot(m), loc.at[4])
    sem_g = take()
    move_g = copy(g_in, gslot(swap_m), swapped, sem_g)
    moves = yh != bit
    pl.when(moves)(lambda: move_g.start())
    pl.when(jnp.logical_not(moves))(lambda: own_g.start())

    def ring(src, slot, size, cuts):
        sem = take(2 * len(cuts))
        half = size // 2
        pieces = [(lo, hi - lo) for lo, hi in zip(cuts, cuts[1:])]

        def begin(k):
            lo, n = pieces[k]
            for way, to in ((0, xs[1]), (1, xs[3])):
                send(src.at[pl.ds(lo, n)], slot(x, lo, n), dev(x_=to), sem + 2 * k + way)

        def first():
            for way, to, came in ((0, xs[1], xs[3]), (1, xs[3], xs[1])):
                for k, (lo, n) in enumerate(pieces):
                    arrived(slot(came, lo, n), sem + 2 * k + way)
                send(slot(came, way * half, half), slot(came, way * half, half), dev(x_=to), sem + 2 * len(pieces) + way)

        def last():
            for way in range(2):
                arrived(slot(xs[2], way * half, half), sem + 2 * len(pieces) + way)

        return begin, first, last

    a_begin, a_first, a_last = ring(a_in, arow, T, (0, T))
    b_begin, b_first, b_last = ring(b_in, lambda xx, lo, n: bslot(xx, c, lo, n), O, (0, O // 4, O))
    sem_l, sem_rd, sem_ld, sem_bd = take(), take(2), take(2), take(4)
    sem_r = take(2)
    r_cut = 640
    mine, other = yh * 2 + c, (1 - yh) * 2 + c

    def r_rows(slot, k):
        return slot.at[pl.ds(k * r_cut, r_cut + k * (I - 2 * r_cut))]

    def r_send(k):
        send(r_rows(r_in, k), r_rows(rbuf.at[mine], k), across, sem_r + k)

    row = lax.broadcasted_iota(jnp.int32, (8, 128), 0)
    tile = jnp.zeros((8, 128), jnp.int32)
    end = 0
    for k in range(SEQ_DEV):
        end = end + sp[0, k]
        tile = jnp.where(row == k, end, tile)
    ends[x] = tile
    sem_e = take(3)
    for k in (1, 2, 3):
        send(ends.at[x], ends.at[x], dev(x_=xs[k]), sem_e + k - 1)
    a_begin(0)
    b_begin(0)
    r_send(0)
    send(r_in, rbuf.at[mine], sibling, sem_rd)
    send(b_in, bslot(x, c), sibling, sem_bd)
    send(l_in, lbuf.at[mine], sibling, sem_ld)
    for cp in own:
        cp.start()

    pl.when(moves)(lambda: copy(g_in, gslot(m), swapped, sem_g).wait_recv())
    pl.when(jnp.logical_not(moves))(lambda: own_g.wait())
    g_begin, g_second, g_go = spread(gslot, T)
    g_begin()
    r_send(1)
    g_go(0, 0)
    g_second()
    a_first()
    b_begin(1)
    g_go(0, 1)
    g_go(1, 0)

    def right(u, cc):
        part = jnp.dot(abuf[...], rbuf[(mine // 2 if u == 0 else other // 2) * 2 + cc], preferred_element_type=F32)
        for a in range(NX):
            pf[u, 2 * a + cc] = part[a * T:(a + 1) * T]

    zs = [(z + k) % NZ for k in (4, 3, 5, 2, 6, 1, 7, 0)]
    sem_y, sem_z = take(6), take(16)
    quarter = H // 2
    keep, give = pl.ds(yl * H, H), pl.ds((1 - yl) * H, H)

    lots = ((0, 1), (1, 2), (3, 5))
    met = set()

    def pair_sum(u):
        for k, zz in enumerate(zs):
            pb[u, k] = pf[u, zz, give].astype(BF16)
            for lot, (first, n) in enumerate(lots):
                if k == first + n - 1:
                    blocks = pl.ds(first, n)
                    send(pb.at[u, blocks], yb.at[u, blocks], beside, sem_y + 3 * u + lot)

    def partial(u, k):
        lot = max(i for i, (first, _) in enumerate(lots) if first <= k)
        if (u, lot) not in met:
            met.add((u, lot))
            arrived(yb.at[u, pl.ds(*lots[lot])], sem_y + 3 * u + lot)
        return pf[u, zs[k], keep] + yb[u, k].astype(F32)

    def hop(u, way, step):
        return sem_z + 8 * u + way * 4 + step

    def z_first(u):
        chunk = partial(u, 0)
        for way, to in enumerate((zr, zl)):
            zsend[u, way, 0, :quarter] = chunk[way * quarter:(way + 1) * quarter]
            send(zsend.at[u, way, 0, pl.ds(0, quarter)], zrecv.at[u, way, 0, pl.ds(0, quarter)], dev(z_=to), hop(u, way, 0))

    def z_next(u, step):
        for way, to in enumerate((zr, zl)):
            chunk = partial(u, 2 * step - 1 + way)
            arrived(zrecv.at[u, way, step - 1, pl.ds(0, quarter if step == 1 else H)], hop(u, way, step - 1))
            if step == 1:
                zsend[u, way, step] = chunk
                rows = pl.ds(way * quarter, quarter)
                zsend[u, way, step, rows] = zsend[u, way, step, rows] + zrecv[u, way, 0, :quarter]
            else:
                zsend[u, way, step] = chunk + zrecv[u, way, step - 1]
            send(zsend.at[u, way, step], zrecv.at[u, way, step], dev(z_=to), hop(u, way, step))

    def z_last(u):
        total = partial(u, 7)
        for way in range(2):
            arrived(zrecv.at[u, way, 3], hop(u, way, 3))
            total = total + zrecv[u, way, 3]
        rfull[u, z, keep] = total.astype(BF16)

    a_last()
    own[0].wait()
    own[3].wait()
    g_go(0, 2)
    right(0, c)
    arrived(rbuf.at[yh * 2 + 1 - c], sem_rd)
    right(0, 1 - c)
    pair_sum(0)
    g_go(1, 1)
    for k in range(2):
        arrived(r_rows(rbuf.at[other], k), sem_r + k)
    send(rbuf.at[other], rbuf.at[other], sibling, sem_rd + 1)
    right(1, c)
    z_first(0)
    arrived(rbuf.at[(1 - yh) * 2 + 1 - c], sem_rd + 1)
    right(1, 1 - c)
    pair_sum(1)
    send(l_in, lbuf.at[mine], across, sem_l)
    b_first()
    send(bslot(xs[3], c), bslot(xs[3], c), sibling, sem_bd + 1)
    send(bslot(xs[1], c), bslot(xs[1], c), sibling, sem_bd + 2)
    g_go(1, 2)
    z_next(0, 1)
    z_first(1)
    z_next(0, 2)
    z_next(1, 1)
    b_last()
    send(bslot(xs[2], c), bslot(xs[2], c), sibling, sem_bd + 3)
    z_next(0, 3)
    z_next(1, 2)
    f0_begin, f0_go, f0_pair = relay(fslot(0), H)
    f1_begin, f1_go, f1_pair = relay(fslot(1), H)

    g_go(0, 3)
    g_go(1, 3)
    own[1].wait()
    for k, xx in enumerate((x, xs[3], xs[1], xs[2])):
        arrived(bslot(xx, 1 - c), sem_bd + k)
    total = jnp.zeros((2 * T, E), F32)
    for j in range(8):
        total = total + jnp.dot(gbuf[j], bbuf[j], preferred_element_type=F32)
    prot[...] = total
    sem_rot, sem_xr = take(2), take(6)
    for p in range(2):
        send(prot.at[pl.ds((1 - yh) * T + p * H, H)], rprot.at[pl.ds(p * H, H)], across, sem_rot + p)

    def rotated(p):
        arrived(rprot.at[pl.ds(p * H, H)], sem_rot + p)
        at = pl.ds(x * T + p * H, H)
        xrot[at] = (prot[pl.ds(yh * T + p * H, H)] + rprot[p * H:(p + 1) * H]).astype(BF16)
        for k in (1, 2, 3):
            send(xrot.at[at], xrot.at[at], dev(x_=xs[k]), sem_xr + 3 * p + k - 1)

    z_next(1, 3)
    z_last(0)
    f0_begin()
    z_last(1)
    f1_begin()
    f0_go(0)
    f0_go(1)
    arrived(lbuf.at[other], sem_l)
    send(lbuf.at[other], lbuf.at[other], sibling, sem_ld + 1)
    rotated(0)
    rotated(1)
    f1_go(0)
    f1_go(1)
    f0_go(2)
    f0_go(3)
    f1_go(2)
    f1_go(3)

    own[2].wait()
    arrived(lbuf.at[yh * 2 + 1 - c], sem_ld)
    arrived(lbuf.at[(1 - yh) * 2 + 1 - c], sem_ld + 1)
    for k in (1, 2, 3):
        for p in range(2):
            arrived(xrot.at[pl.ds(xs[4 - k] * T + p * H, H)], sem_xr + 3 * p + k - 1)
        arrived(ends.at[xs[4 - k]], sem_e + k - 1)
    for u in range(2):
        for cc in range(2):
            slot_of = (mine // 2 if u == 0 else other // 2) * 2 + cc
            part = jnp.dot(xrot[...], lbuf[slot_of], preferred_element_type=F32)
            for a in range(NX):
                left[u, 2 * a + cc] = part[a * T:(a + 1) * T]

    token = lax.broadcasted_iota(jnp.int32, (T, C), 0)

    def product(u, zz):
        prod = left[u, zz] * rfull[u, zz].astype(F32)
        stops = ends[zz // 2]
        below = [token < jnp.broadcast_to(stops[k:k + 1, :1], (T, C)) for k in range(SEQ_DEV)]
        rows = []
        for k in range(SEQ_DEV):
            inside = below[0] if k == 0 else below[k] & jnp.logical_not(below[k - 1])
            rows.append(jnp.sum(jnp.where(inside, prod, 0.0), axis=0, keepdims=True))
        at = (u * NZ + zz) * 8
        sbuf[pl.ds(pl.multiple_of(at, 8), 8)] = jnp.concatenate(rows + [jnp.zeros((8 - SEQ_DEV, C), F32)], axis=0)

    sem_s = take(NM)
    column, query = (lax.broadcasted_iota(jnp.int32, (C, 128), k) for k in (0, 1))
    ranks = (column // RANK == query).astype(F32)
    finals = []
    for u, pair in enumerate((f0_pair, f1_pair)):
        for k in range(-1, 4):
            pair(k)
            for far in {-1: (0,), 3: (4,)}.get(k, (k + 1, NZ - 1 - k)):
                product(u, (z + far) % NZ)
        tiles = jnp.dot(sbuf[u * 64:(u + 1) * 64], ranks, precision=lax.Precision.HIGHEST, preferred_element_type=F32)
        for zz in range(NZ):
            n = u * NZ + zz
            ssend[n] = tiles[zz * 8:(zz + 1) * 8]
            to_d, to_m = 4 * (zz // 2) + 2 * yh + c, 4 * x + (mine // 2 if u == 0 else other // 2) * 2 + zz % 2
            here = (to_d == d) & (to_m == m)
            cp = copy(ssend.at[n], srecv.at[m], (to_d, to_m), sem_s + n, sem_s + m)
            finals.append((here, cp))
            pl.when(jnp.logical_not(here))(cp.start)

            @pl.when(here)
            def _():
                srecv[m] = ssend[n]

    for src in range(NM):
        pl.when(jnp.logical_not((x == m // 4) & (m == src)))(functools.partial(arrived, srecv.at[src], sem_s + src))
    scores = srecv[0]
    for src in range(1, NM):
        scores = scores + srecv[src]
    scores = scores * (1.0 / jnp.sqrt(jnp.float32(RANK * TOK_DEV)))
    out[...] = scores[:SEQ_DEV, :C // RANK]

    for cp in sent:
        cp.wait_send()
    pl.when(moves)(lambda: move_g.wait_send())
    for here, cp in finals:
        pl.when(jnp.logical_not(here))(cp.wait_send)
    assert used[0] <= NSEM, used[0]


NSEM = 160


def on_device(out_grads, basis, left_factors, right_factors, activations, spans):
    vmem = pltpu.VMEM
    return pl.pallas_call(
        kernel,
        out_shape=jax.ShapeDtypeStruct((SEQ_DEV, C // RANK), F32),
        in_specs=[pl.BlockSpec(memory_space=pltpu.HBM)] * 5 + [pl.BlockSpec(memory_space=pltpu.SMEM)],
        out_specs=pl.BlockSpec(memory_space=vmem),
        scratch_shapes=[
            vmem((8, 2 * T, O), BF16),
            vmem((8, O, E), BF16),
            vmem((4, E, C), BF16),
            vmem((4, I, C), BF16),
            vmem((NX * T, I), BF16),
            vmem((2 * T, E), F32),
            vmem((T, E), F32),
            vmem((NX * T, E), BF16),
            vmem((2, NZ, T, C), F32),
            vmem((2, NZ, H, C), BF16),
            vmem((2, NZ, H, C), BF16),
            vmem((2, 2, 4, H, C), F32),
            vmem((2, 2, 4, H, C), F32),
            vmem((2, NZ, T, C), BF16),
            vmem((2, NZ, T, C), F32),
            vmem((NX, 8, 128), jnp.int32),
            vmem((NM * 8, C), F32),
            vmem((NM, 8, 128), F32),
            vmem((NM, 8, 128), F32),
            pltpu.SemaphoreType.DMA((5,)),
            pltpu.SemaphoreType.DMA((NSEM,)),
            pltpu.SemaphoreType.DMA((NSEM,)),
        ],
        compiler_params=pltpu.CompilerParams(collective_id=0, has_side_effects=True, vmem_limit_bytes=60 << 20),
    )(out_grads, basis, left_factors, right_factors, activations, spans)


def solution(mesh):
    placed = (
        P("dp", "mp"),
        P("dp", "mp"),
        P("mp", "dp"),
        P("mp", "dp"),
        P("dp", "mp"),
        P("dp", None),
    )
    return jax.shard_map(
        on_device, mesh=mesh, in_specs=placed, out_specs=P("dp", "mp"), check_vma=False
    )
```

```python
import functools

import jax
import jax.numpy as jnp
from jax import lax
from jax.experimental import pallas as pl
from jax.experimental.pallas import tpu as pltpu
from jax.sharding import PartitionSpec as P

RANK = 32
TOK_DEV = 128
SEQ_DEV = 4
MESH = pl.DeviceIdType.MESH
BF16, F32 = jnp.bfloat16, jnp.float32

NX, NZ, NM = 4, 8, 16
T, O, E, C, I = 128, 512, 512, 256, 1792
H = T // 2


def kernel(g_in, b_in, l_in, r_in, a_in, sp, out, gbuf, bbuf, lbuf, rbuf, abuf, prot, rprot, xrot, pf, pb, yb, zsend, zrecv,
           rfull, left, ends, sbuf, ssend, srecv, loc, ss, rs):
    d, m = lax.axis_index("dp"), lax.axis_index("mp")
    x, yh, c = d // 4, (d // 2) % 2, d % 2
    yl, z = m // NZ, m % NZ

    def dev(x_=None, yh_=None, c_=None, yl_=None, z_=None):
        pick = lambda new, old: old if new is None else new
        return (4 * pick(x_, x) + 2 * pick(yh_, yh) + pick(c_, c), NZ * pick(yl_, yl) + pick(z_, z))

    xs = [(x + k) % NX for k in range(NX)]
    zr, zl = (z + 1) % NZ, (z + NZ - 1) % NZ
    sibling, across, beside = dev(c_=1 - c), dev(yh_=1 - yh), dev(yl_=1 - yl)
    bit = (m // 2) % 2
    swap_m = m + 2 - 4 * bit
    swapped = (4 * x + 2 * (1 - yh) + c, swap_m)

    def greet(to):
        pl.semaphore_signal(pltpu.get_barrier_semaphore(), inc=1, device_id=to, device_id_type=MESH)

    near = [dev(x_=xs[k]) for k in (1, 2, 3)] + [dev(z_=zr), dev(z_=zl), sibling, across, beside, swapped]
    for to in near:
        greet(to)
    pl.semaphore_wait(pltpu.get_barrier_semaphore(), len(near))

    used = [0]

    def take(n=1):
        used[0] += n
        return used[0] - n

    sent = []

    def copy(src, dst, to, sem, sem_there=None):
        sem_there = sem if sem_there is None else sem_there
        return pltpu.make_async_remote_copy(
            src_ref=src, dst_ref=dst, send_sem=ss.at[sem], recv_sem=rs.at[sem_there], device_id=to, device_id_type=MESH
        )

    def send(src, dst, to, sem):
        cp = copy(src, dst, to, sem)
        cp.start()
        sent.append(cp)

    def arrived(dst, sem):
        copy(dst, dst, sibling, sem).wait_recv()

    def gslot(mm, lo=0, n=T):
        return gbuf.at[(mm // 4) * 2 + mm % 2, pl.ds(((mm // 2) % 2) * T + lo, n)]

    def fslot(u):
        return lambda mm, lo=0, n=H: rfull.at[u, mm % NZ, pl.ds((mm // NZ) * H + lo, n)]

    def arow(xx, lo=0, n=T):
        return abuf.at[pl.ds(xx * T + lo, n)]

    def bslot(xx, cc, lo=0, n=O):
        return bbuf.at[xx * 2 + cc, pl.ds(lo, n)]

    def spread(slot, rows):
        sem_pair, sem = take(), take(16)
        half = rows // 2

        def at(stream, direction, step):
            return sem + stream * 8 + direction * 4 + step

        def stage(stream, step):
            row = yl if stream == 0 else 1 - yl
            for direction, (to, sign) in enumerate(((zr, -1), (zl, 1))):
                origin = row * NZ + (z + sign * step + NZ) % NZ
                lo, n = (0, rows) if step < 3 else (half * direction, half)
                send(slot(origin, lo, n), slot(origin, lo, n), dev(z_=to), at(stream, direction, step))

        def landed(stream, step):
            row = yl if stream == 0 else 1 - yl
            for direction, sign in ((0, -1), (1, 1)):
                origin = row * NZ + (z + sign * (step + 1) + NZ) % NZ
                lo, n = (0, rows) if step < 3 else (half * direction, half)
                arrived(slot(origin, lo, n), at(stream, direction, step))

        def begin():
            send(slot(m), slot(m), beside, sem_pair)
            stage(0, 0)

        def second():
            arrived(slot((1 - yl) * NZ + z), sem_pair)
            stage(1, 0)

        def go(stream, k):
            landed(stream, k)
            if k < 3:
                stage(stream, k + 1)

        return begin, second, go

    def relay(slot, rows):
        sem, half = take(17), rows // 2

        def piece(row, direction, step):
            origin = row * NZ + (z + (-step, step)[direction] + NZ) % NZ
            return slot(origin, 0, rows) if step < 4 else slot(origin, half * direction, half)

        def begin():
            for far in (1, 2):
                for direction in range(2):
                    to = dev(z_=(z + (far, NZ - far)[direction]) % NZ)
                    send(slot(m), slot(m), to, sem + 2 * (far - 1) + direction)
            send(slot(m), slot(m), beside, sem + 16)

        def go(k):
            for direction in range(2):
                block = piece(yl, direction, k + 1)
                arrived(block, sem + 2 * k + direction)
                if k == 1:
                    send(block, block, dev(z_=(zr, zl)[direction]), sem + 4 + direction)
                    part = slot(yl * NZ + (z + (-2, 2)[direction] + NZ) % NZ, half * direction, half)
                    send(part, part, dev(z_=(z + (2, NZ - 2)[direction]) % NZ), sem + 6 + direction)
                send(block, block, beside, sem + 8 + 2 * k + direction)

        def pair(k):
            if k < 0:
                arrived(slot((1 - yl) * NZ + z), sem + 16)
            else:
                for direction in range(2):
                    arrived(piece(1 - yl, direction, k + 1), sem + 8 + 2 * k + direction)

        return begin, go, pair

    places = [(a_in, arow(x)), (b_in, bslot(x, c)), (l_in, lbuf.at[yh * 2 + c]), (r_in, rbuf.at[yh * 2 + c])]
    own = [pltpu.make_async_copy(src, dst, loc.at[i]) for i, (src, dst) in enumerate(places)]
    own_g = pltpu.make_async_copy(g_in, gslot(m), loc.at[4])
    sem_g = take()
    move_g = copy(g_in, gslot(swap_m), swapped, sem_g)
    moves = yh != bit
    pl.when(moves)(lambda: move_g.start())
    pl.when(jnp.logical_not(moves))(lambda: own_g.start())

    def ring(src, slot, size, cuts):
        sem = take(2 * len(cuts))
        half = size // 2
        pieces = [(lo, hi - lo) for lo, hi in zip(cuts, cuts[1:])]

        def begin(k):
            lo, n = pieces[k]
            for way, to in ((0, xs[1]), (1, xs[3])):
                send(src.at[pl.ds(lo, n)], slot(x, lo, n), dev(x_=to), sem + 2 * k + way)

        def first():
            for way, to, came in ((0, xs[1], xs[3]), (1, xs[3], xs[1])):
                for k, (lo, n) in enumerate(pieces):
                    arrived(slot(came, lo, n), sem + 2 * k + way)
                send(slot(came, way * half, half), slot(came, way * half, half), dev(x_=to), sem + 2 * len(pieces) + way)

        def last():
            for way in range(2):
                arrived(slot(xs[2], way * half, half), sem + 2 * len(pieces) + way)

        return begin, first, last

    a_begin, a_first, a_last = ring(a_in, arow, T, (0, T))
    b_begin, b_first, b_last = ring(b_in, lambda xx, lo, n: bslot(xx, c, lo, n), O, (0, O // 4, O))
    sem_l, sem_rd, sem_ld, sem_bd = take(), take(3), take(2), take(4)
    sem_r = take(2)
    r_cut = 640
    mine, other = yh * 2 + c, (1 - yh) * 2 + c

    def r_rows(slot, k):
        return slot.at[pl.ds(k * r_cut, r_cut + k * (I - 2 * r_cut))]

    def r_send(k):
        send(r_rows(r_in, k), r_rows(rbuf.at[mine], k), across, sem_r + k)

    def r_pass(k):
        arrived(r_rows(rbuf.at[other], k), sem_r + k)
        send(r_rows(rbuf.at[other], k), r_rows(rbuf.at[other], k), sibling, sem_rd + 1 + k)

    row = lax.broadcasted_iota(jnp.int32, (8, 128), 0)
    tile = jnp.zeros((8, 128), jnp.int32)
    end = 0
    for k in range(SEQ_DEV):
        end = end + sp[0, k]
        tile = jnp.where(row == k, end, tile)
    ends[x] = tile
    sem_e = take(3)
    for k in (1, 2, 3):
        send(ends.at[x], ends.at[x], dev(x_=xs[k]), sem_e + k - 1)
    a_begin(0)
    b_begin(0)
    r_send(0)
    send(r_in, rbuf.at[mine], sibling, sem_rd)
    send(b_in, bslot(x, c), sibling, sem_bd)
    send(l_in, lbuf.at[mine], sibling, sem_ld)
    for cp in own:
        cp.start()

    pl.when(moves)(lambda: copy(g_in, gslot(m), swapped, sem_g).wait_recv())
    pl.when(jnp.logical_not(moves))(lambda: own_g.wait())
    g_begin, g_second, g_go = spread(gslot, T)
    g_begin()
    r_send(1)
    g_go(0, 0)
    g_second()
    a_first()
    b_begin(1)
    g_go(0, 1)
    g_go(1, 0)
    r_pass(0)

    def right(u, cc):
        part = jnp.dot(abuf[...], rbuf[(mine // 2 if u == 0 else other // 2) * 2 + cc], preferred_element_type=F32)
        for a in range(NX):
            pf[u, 2 * a + cc] = part[a * T:(a + 1) * T]

    zs = [(z + k) % NZ for k in (4, 3, 5, 2, 6, 1, 7, 0)]
    sem_y, sem_z = take(6), take(16)
    quarter = H // 2
    keep, give = pl.ds(yl * H, H), pl.ds((1 - yl) * H, H)

    lots = ((0, 1), (1, 2), (3, 5))
    met = set()

    def pair_sum(u):
        for k, zz in enumerate(zs):
            pb[u, k] = pf[u, zz, give].astype(BF16)
            for lot, (first, n) in enumerate(lots):
                if k == first + n - 1:
                    blocks = pl.ds(first, n)
                    send(pb.at[u, blocks], yb.at[u, blocks], beside, sem_y + 3 * u + lot)

    def partial(u, k):
        lot = max(i for i, (first, _) in enumerate(lots) if first <= k)
        if (u, lot) not in met:
            met.add((u, lot))
            arrived(yb.at[u, pl.ds(*lots[lot])], sem_y + 3 * u + lot)
        return pf[u, zs[k], keep] + yb[u, k].astype(F32)

    def hop(u, way, step):
        return sem_z + 8 * u + way * 4 + step

    def z_first(u):
        chunk = partial(u, 0)
        for way, to in enumerate((zr, zl)):
            zsend[u, way, 0, :quarter] = chunk[way * quarter:(way + 1) * quarter]
            send(zsend.at[u, way, 0, pl.ds(0, quarter)], zrecv.at[u, way, 0, pl.ds(0, quarter)], dev(z_=to), hop(u, way, 0))

    def z_next(u, step):
        for way, to in enumerate((zr, zl)):
            chunk = partial(u, 2 * step - 1 + way)
            arrived(zrecv.at[u, way, step - 1, pl.ds(0, quarter if step == 1 else H)], hop(u, way, step - 1))
            if step == 1:
                zsend[u, way, step] = chunk
                rows = pl.ds(way * quarter, quarter)
                zsend[u, way, step, rows] = zsend[u, way, step, rows] + zrecv[u, way, 0, :quarter]
            else:
                zsend[u, way, step] = chunk + zrecv[u, way, step - 1]
            send(zsend.at[u, way, step], zrecv.at[u, way, step], dev(z_=to), hop(u, way, step))

    def z_last(u):
        total = partial(u, 7)
        for way in range(2):
            arrived(zrecv.at[u, way, 3], hop(u, way, 3))
            total = total + zrecv[u, way, 3]
        rfull[u, z, keep] = total.astype(BF16)

    a_last()
    own[0].wait()
    own[3].wait()
    g_go(0, 2)
    right(0, c)
    arrived(rbuf.at[yh * 2 + 1 - c], sem_rd)
    right(0, 1 - c)
    pair_sum(0)
    g_go(1, 1)
    r_pass(1)
    right(1, c)
    z_first(0)
    for k in range(2):
        arrived(r_rows(rbuf.at[(1 - yh) * 2 + 1 - c], k), sem_rd + 1 + k)
    right(1, 1 - c)
    pair_sum(1)
    send(l_in, lbuf.at[mine], across, sem_l)
    b_first()
    send(bslot(xs[3], c), bslot(xs[3], c), sibling, sem_bd + 1)
    send(bslot(xs[1], c), bslot(xs[1], c), sibling, sem_bd + 2)
    g_go(1, 2)
    z_next(0, 1)
    z_first(1)
    z_next(0, 2)
    z_next(1, 1)
    b_last()
    send(bslot(xs[2], c), bslot(xs[2], c), sibling, sem_bd + 3)
    z_next(0, 3)
    z_next(1, 2)
    f0_begin, f0_go, f0_pair = relay(fslot(0), H)
    f1_begin, f1_go, f1_pair = relay(fslot(1), H)

    g_go(0, 3)
    g_go(1, 3)
    own[1].wait()
    for k, xx in enumerate((x, xs[3], xs[1], xs[2])):
        arrived(bslot(xx, 1 - c), sem_bd + k)
    total = jnp.zeros((2 * T, E), F32)
    for j in range(8):
        total = total + jnp.dot(gbuf[j], bbuf[j], preferred_element_type=F32)
    prot[...] = total
    sem_rot, sem_xr = take(2), take(6)
    for p in range(2):
        send(prot.at[pl.ds((1 - yh) * T + p * H, H)], rprot.at[pl.ds(p * H, H)], across, sem_rot + p)

    def rotated(p):
        arrived(rprot.at[pl.ds(p * H, H)], sem_rot + p)
        at = pl.ds(x * T + p * H, H)
        xrot[at] = (prot[pl.ds(yh * T + p * H, H)] + rprot[p * H:(p + 1) * H]).astype(BF16)
        for k in (1, 2, 3):
            send(xrot.at[at], xrot.at[at], dev(x_=xs[k]), sem_xr + 3 * p + k - 1)

    z_next(1, 3)
    z_last(0)
    f0_begin()
    z_last(1)
    f1_begin()
    f0_go(0)
    f0_go(1)
    arrived(lbuf.at[other], sem_l)
    send(lbuf.at[other], lbuf.at[other], sibling, sem_ld + 1)
    rotated(0)
    rotated(1)
    f1_go(0)
    f1_go(1)
    f0_go(2)
    f0_go(3)
    f1_go(2)
    f1_go(3)

    own[2].wait()
    arrived(lbuf.at[yh * 2 + 1 - c], sem_ld)
    arrived(lbuf.at[(1 - yh) * 2 + 1 - c], sem_ld + 1)
    for k in (1, 2, 3):
        for p in range(2):
            arrived(xrot.at[pl.ds(xs[4 - k] * T + p * H, H)], sem_xr + 3 * p + k - 1)
        arrived(ends.at[xs[4 - k]], sem_e + k - 1)
    for u in range(2):
        for cc in range(2):
            slot_of = (mine // 2 if u == 0 else other // 2) * 2 + cc
            part = jnp.dot(xrot[...], lbuf[slot_of], preferred_element_type=F32)
            for a in range(NX):
                left[u, 2 * a + cc] = part[a * T:(a + 1) * T]

    token = lax.broadcasted_iota(jnp.int32, (T, C), 0)

    def product(u, zz):
        prod = left[u, zz] * rfull[u, zz].astype(F32)
        stops = ends[zz // 2]
        below = [token < jnp.broadcast_to(stops[k:k + 1, :1], (T, C)) for k in range(SEQ_DEV)]
        rows = []
        for k in range(SEQ_DEV):
            inside = below[0] if k == 0 else below[k] & jnp.logical_not(below[k - 1])
            rows.append(jnp.sum(jnp.where(inside, prod, 0.0), axis=0, keepdims=True))
        at = (u * NZ + zz) * 8
        sbuf[pl.ds(pl.multiple_of(at, 8), 8)] = jnp.concatenate(rows + [jnp.zeros((8 - SEQ_DEV, C), F32)], axis=0)

    sem_s = take(NM)
    column, query = (lax.broadcasted_iota(jnp.int32, (C, 128), k) for k in (0, 1))
    ranks = (column // RANK == query).astype(F32)
    finals = []
    for u, pair in enumerate((f0_pair, f1_pair)):
        for k in range(-1, 4):
            pair(k)
            for far in {-1: (0,), 3: (4,)}.get(k, (k + 1, NZ - 1 - k)):
                product(u, (z + far) % NZ)
        tiles = jnp.dot(sbuf[u * 64:(u + 1) * 64], ranks, precision=lax.Precision.HIGHEST, preferred_element_type=F32)
        for zz in range(NZ):
            n = u * NZ + zz
            ssend[n] = tiles[zz * 8:(zz + 1) * 8]
            to_d, to_m = 4 * (zz // 2) + 2 * yh + c, 4 * x + (mine // 2 if u == 0 else other // 2) * 2 + zz % 2
            here = (to_d == d) & (to_m == m)
            cp = copy(ssend.at[n], srecv.at[m], (to_d, to_m), sem_s + n, sem_s + m)
            finals.append((here, cp))
            pl.when(jnp.logical_not(here))(cp.start)

            @pl.when(here)
            def _():
                srecv[m] = ssend[n]

    for src in range(NM):
        pl.when(jnp.logical_not((x == m // 4) & (m == src)))(functools.partial(arrived, srecv.at[src], sem_s + src))
    scores = srecv[0]
    for src in range(1, NM):
        scores = scores + srecv[src]
    scores = scores * (1.0 / jnp.sqrt(jnp.float32(RANK * TOK_DEV)))
    out[...] = scores[:SEQ_DEV, :C // RANK]

    for cp in sent:
        cp.wait_send()
    pl.when(moves)(lambda: move_g.wait_send())
    for here, cp in finals:
        pl.when(jnp.logical_not(here))(cp.wait_send)
    assert used[0] <= NSEM, used[0]


NSEM = 160


def on_device(out_grads, basis, left_factors, right_factors, activations, spans):
    vmem = pltpu.VMEM
    return pl.pallas_call(
        kernel,
        out_shape=jax.ShapeDtypeStruct((SEQ_DEV, C // RANK), F32),
        in_specs=[pl.BlockSpec(memory_space=pltpu.HBM)] * 5 + [pl.BlockSpec(memory_space=pltpu.SMEM)],
        out_specs=pl.BlockSpec(memory_space=vmem),
        scratch_shapes=[
            vmem((8, 2 * T, O), BF16),
            vmem((8, O, E), BF16),
            vmem((4, E, C), BF16),
            vmem((4, I, C), BF16),
            vmem((NX * T, I), BF16),
            vmem((2 * T, E), F32),
            vmem((T, E), F32),
            vmem((NX * T, E), BF16),
            vmem((2, NZ, T, C), F32),
            vmem((2, NZ, H, C), BF16),
            vmem((2, NZ, H, C), BF16),
            vmem((2, 2, 4, H, C), F32),
            vmem((2, 2, 4, H, C), F32),
            vmem((2, NZ, T, C), BF16),
            vmem((2, NZ, T, C), F32),
            vmem((NX, 8, 128), jnp.int32),
            vmem((NM * 8, C), F32),
            vmem((NM, 8, 128), F32),
            vmem((NM, 8, 128), F32),
            pltpu.SemaphoreType.DMA((5,)),
            pltpu.SemaphoreType.DMA((NSEM,)),
            pltpu.SemaphoreType.DMA((NSEM,)),
        ],
        compiler_params=pltpu.CompilerParams(collective_id=0, has_side_effects=True, vmem_limit_bytes=60 << 20),
    )(out_grads, basis, left_factors, right_factors, activations, spans)


def solution(mesh):
    placed = (
        P("dp", "mp"),
        P("dp", "mp"),
        P("mp", "dp"),
        P("mp", "dp"),
        P("dp", "mp"),
        P("dp", None),
    )
    return jax.shard_map(
        on_device, mesh=mesh, in_specs=placed, out_specs=P("dp", "mp"), check_vma=False
    )
```
